128 devices in a mesh: tm: 32 (over y, z, core), space: 4 (over x).
Axes of the slice: x: 4, y: 4, z: 4, core: 2. Of those that a mesh axis runs over, the one named last changes fastest.
Arguments:
- iterate: float32 [32, 2, 128, 1024], P('tm', None, 'space'), may hold values from -1.6 to 1.6, as said below
Outputs:
- coarse_iterate: float32 [32, 2, 128, 1024], P('tm', None, 'space')
- residual: float32 [32, 2, 128, 1024], P('tm', None, 'space')
The draws below stay inside these ranges and needn't reach their ends.
Inputs may be any that keep to these rules, and one draw needn't show every extreme that they name: `iterate`: row 0 holds the initial condition.
All inputs are finite; a program needn't handle non-finite values.
Results may differ from the reference program's by a relative error of at most 0.00002.
Values sent between devices are 32-bit elements; how exact they have to be, the bound alone decides.
A program may use at most 64 MiB of HBM per device.

```python
import math
import jax
import jax.numpy as jnp
from jax import lax

COLS = 1024
M = 16
NR = 128
NC = 32


def draw_iterate(key, part):
    key = jax.random.fold_in(key, 11)
    subkeys = jax.random.split(key, 5)
    row_index = jnp.arange(NR, dtype=jnp.float32)
    column_index = jnp.arange(COLS, dtype=jnp.float32)
    column_waves = jax.random.randint(subkeys[0], (4,), 1, 9).astype(jnp.float32)
    row_waves = jax.random.randint(subkeys[1], (4,), 1, 7).astype(jnp.float32)
    phases = jax.random.uniform(subkeys[2], (4,), jnp.float32, -math.pi, math.pi)
    reach = 0.3
    amplitude = jax.random.uniform(subkeys[3], (NC, 2, 4), jnp.float32, -reach, reach)
    field = jnp.zeros((NC, 2, NR, COLS), jnp.float32)
    for mode_index in range(4):
        row_shape = jnp.sin(math.pi * row_waves[mode_index] * (row_index + 1.0) / (NR + 1.0))
        column_shape = jnp.sin(2.0 * math.pi * column_waves[mode_index] * column_index / COLS + phases[mode_index])
        field = field + amplitude[:, :, mode_index, None, None] * (row_shape[:, None] * column_shape[None, :])
    rough = jax.random.uniform(subkeys[4], (NC, 2, NR, COLS), jnp.float32, -0.4, 0.4)
    field = field + rough
    return field


def setup_inputs(seed: int = 0) -> dict:
    key_list = jax.random.split(jax.random.key(seed), 2)
    return {
        "iterate": draw_iterate(jax.random.fold_in(key_list[1], 71), 0),
    }


viscosity = 0.8
time_step = 0.015625


def tendency(padded):
    center = padded[..., 1:-1, :]
    above = padded[..., 2:, :]
    below = padded[..., :-2, :]
    left_cells = jnp.roll(center, 1, axis=-1)
    right_cells = jnp.roll(center, -1, axis=-1)
    slope_x = 0.5 * (right_cells - left_cells)
    slope_y = 0.5 * (above - below)
    laplace = (above + below) + (left_cells + right_cells) - 4.0 * center
    advect = center[..., 0:1, :, :] * slope_x + center[..., 1:2, :, :] * slope_y
    return viscosity * laplace - advect


def pad_rows(state):
    widths = [(0, 0)] * (state.ndim - 2) + [(1, 1), (0, 0)]
    return jnp.pad(state, widths)


def heun_step(state, step):
    middle = state + step * tendency(pad_rows(state))
    return 0.5 * (state + middle + step * tendency(pad_rows(middle)))


def propagate(state, count):
    return lax.fori_loop(0, count, lambda index, value: heun_step(value, time_step), state)


def reference(iterate):
    relaxed = propagate(iterate, M)
    restart = jnp.concatenate([iterate[0:1], relaxed[:-1]], axis=0)
    propagated = propagate(restart, M)
    residual = propagated - relaxed
    coarse_step = time_step * M
    terms = propagated - heun_step(restart, coarse_step)

    def chain(state, term):
        updated = heun_step(state, coarse_step) + term
        return updated, updated

    final_state, coarse_iterate = lax.scan(chain, iterate[0], terms)
    return coarse_iterate, residual
```

```python
import jax
import jax.numpy as jnp
from jax import lax
from jax.experimental import pallas as pl
from jax.experimental.pallas import tpu as pltpu
from jax.sharding import PartitionSpec as P

MESH = pl.DeviceIdType.MESH
F32 = jnp.float32
H = 0.015625
SCALE = H / 2
VISC = 0.8
FINE = (1.0 - 4.0 * VISC * H, VISC * H, 1.0)
COARSE = (1.0 - 64.0 * VISC * H, 16.0 * VISC * H, 16.0)
WINDOW = 384
OFF = 8
ROWS = 432
B = 32
HALO = 64
GW = B + 2 * HALO


def stage(src, o, masks, consts):
    c0, k, q = consts
    u = src[0, pl.ds(o, 8), :]
    v = src[1, pl.ds(o, 8), :]
    su, sv = (u, v) if q == 1.0 else (q * u, q * v)
    a, b = k - su, k + su
    c = jnp.where(masks[0], k - sv, 0.0)
    d = jnp.where(masks[1], k + sv, 0.0)
    out = []
    for i, x in ((0, u), (1, v)):
        east = src[i, pl.ds(o + 1, 8), :]
        west = src[i, pl.ds(o - 1, 8), :]
        north = pltpu.roll(x, 127, 1)
        south = pltpu.roll(x, 1, 1)
        out.append((c0 * x + a * east) + (b * west + c * north) + d * south)
    return out


def heun(src, mid, dst, start, n1, n2, masks, consts, dst_shift=0, extra=None):
    for i in range(n1):
        o = start - 1 + 8 * i
        m = stage(src, o, masks, consts)
        for c in range(2):
            mid[c, pl.ds(o, 8), :] = m[c]
    for i in range(n2):
        o = start + 8 * i
        m = stage(mid, o, masks, consts)
        for c in range(2):
            new = 0.5 * (src[c, pl.ds(o, 8), :] + m[c])
            if extra is not None:
                new = new + extra(c, o)
            dst[c, pl.ds(o + dst_shift, 8), :] = new


def fine_steps(first, count, even, odd, mid, masks):
    for g in range(first, first + count, 8):
        n1 = (WINDOW - 2 - 4 * g + 7) // 8
        n2 = (WINDOW - 4 - 4 * g + 7) // 8

        def body(t, _):
            for p, (src, dst) in enumerate(((even, odd), (odd, even))):
                start = OFF + 2 * (2 * t + p) + 2
                heun(src, mid, dst, start, n1, n2, masks, FINE)
            return 0

        lax.fori_loop(g // 2, g // 2 + 4, body, 0)


def halo_of(j):
    return 16 * ((30 - j + 7) // 8)


CLASSES = ((0, 6, 64), (6, 14, 48), (14, 22, 32), (22, 30, 16), (30, 31, 0))


def worker_tm(r):
    y = r // 2
    return y * 8 + (2 * (r % 2) + y % 2) * 2


def kernel(
    x_ref, coarse_ref, resid_ref,
    rot, win, abuf, bbuf, dbuf, mid, cbuf, terms, relin, got, s0, s1, smid, ret, back, nres,
    xs, xr, ysem, rels, relr, gs, gr, rets, retr, ress, resr, row0s, row0r,
):
    j = lax.axis_index("tm")
    s = lax.axis_index("space")
    y, q = j // 8, lax.rem(j, 8)
    lane = lax.broadcasted_iota(jnp.int32, (8, 128), 1)
    masks = (lane < 127, lane > 0)

    low = lax.broadcasted_iota(jnp.int32, (32, 128), 1) < 64
    for c in range(2):
        turned = [pltpu.roll(x_ref[0, c, :, 128 * t : 128 * t + 128], 64, 1) for t in range(8)]
        for t in range(9):
            rot[c, :, 128 * t : 128 * t + 128] = jnp.where(low, turned[(t - 1) % 8], turned[t % 8])

    barrier = pltpu.get_barrier_semaphore()
    ring_x = [(j, lax.rem(s + d, 4)) for d in (1, 2, 3)]
    ring_y = [(lax.rem(y + d, 4) * 8 + q, s) for d in (1, 2, 3)]
    plane = [(y * 8 + lax.rem(q + d, 8), s) for d in range(1, 8)]
    for other in ring_x + ring_y + plane:
        pl.semaphore_signal(barrier, inc=1, device_id=other, device_id_type=MESH)
    pl.semaphore_wait(barrier, 13)

    sends = []
    for d in (1, 2, 3):
        to = lax.rem(s + d, 4)
        cp = pltpu.make_async_remote_copy(
            src_ref=rot.at[:, :, pl.ds(pl.multiple_of(256 * to, 128), WINDOW)],
            dst_ref=win.at[s],
            send_sem=xs.at[d - 1],
            recv_sem=xr.at[d - 1],
            device_id=(j, to),
            device_id_type=MESH,
        )
        cp.start()
        sends.append(cp)
    win[s] = rot[:, :, pl.ds(pl.multiple_of(256 * s, 128), WINDOW)]
    for cp in sends:
        cp.wait()
    for other in ring_y:
        pl.semaphore_signal(ysem, inc=1, device_id=other, device_id_type=MESH)
    for c in range(2):
        for t in range(3):
            tile = jnp.concatenate([win[i, c, :, 128 * t : 128 * t + 128] for i in range(4)], axis=0)
            abuf[c, OFF + 128 * t : OFF + 128 * t + 128, :] = tile.T * SCALE

    fine_steps(0, 16, abuf, bbuf, mid, masks)

    pl.semaphore_wait(ysem, 3)
    own = pl.ds(OFF + 64, 256)
    before = pltpu.make_async_remote_copy(
        src_ref=abuf.at[:, own, :], dst_ref=relin, send_sem=rels, recv_sem=relr,
        device_id=(lax.rem(j + 31, 32), s), device_id_type=MESH,
    )
    before.start()

    heun(abuf, mid, cbuf, OFF + 64, 33, 32, masks, COARSE, dst_shift=-(OFF + 64))
    for c in range(2):
        dbuf[c, :, :] = abuf[c, :, :]
    fine_steps(16, 16, dbuf, bbuf, mid, masks)

    for i in range(32):
        for c in range(2):
            rows = pl.ds(8 * i, 8)
            coarse = jnp.where(j > 0, cbuf[c, rows, :], 0.0)
            terms[c, rows, :] = dbuf[c, pl.ds(OFF + 64 + 8 * i, 8), :] - coarse

    def gather(act):
        for first, last, h in CLASSES:

            def pieces(h=h):
                for r in range(-2, 10):
                    lo, hi = max(0, B * r - h), min(256, B * r + B + h)
                    if hi <= lo:
                        continue
                    at = lo - (B * r - HALO)
                    src = terms.at[:, pl.ds(lo, hi - lo), :]
                    dst = got.at[j, :, pl.ds(at, hi - lo), :]
                    holder = worker_tm(r % 8)
                    to = lax.rem(s + (r // 8) + 4, 4)

                    def remote(src=src, dst=dst, r=r, holder=holder, to=to):
                        act(
                            pltpu.make_async_remote_copy(
                                src_ref=src, dst_ref=dst, send_sem=gs.at[r + 2], recv_sem=gr.at[j],
                                device_id=(holder, to), device_id_type=MESH,
                            ),
                            True,
                        )

                    if 0 <= r < 8:
                        pl.when(j != holder)(remote)

                        @pl.when(j == holder)
                        def _(src=src, dst=dst):
                            act(pltpu.make_async_copy(src, dst, gr.at[j]), False)
                    else:
                        remote()

            pl.when((j >= first) & (j < last))(pieces)

    def start(copy, remote):
        copy.start()

    gather(start)

    before.wait()

    @pl.when(j < 31)
    def _():
        for c in range(2):
            for t in range(2):
                rows = pl.ds(OFF + 64 + 128 * t, 128)
                diff = (dbuf[c, rows, :] - relin[c, 128 * t : 128 * t + 128, :]) * (1.0 / SCALE)
                diff = diff.T
                for i in range(4):
                    nres[i, c, :, 128 * t : 128 * t + 128] = diff[32 * i : 32 * i + 32, :]

    @pl.when(j == 31)
    def _():
        for c in range(2):
            for t in range(2):
                for i in range(4):
                    nres[i, c, :, 128 * t : 128 * t + 128] = jnp.zeros((32, 128), F32)

    columns = pl.ds(pl.multiple_of(256 * s, 128), 256)
    res_copies = []
    for i in range(4):
        cp = pltpu.make_async_remote_copy(
            src_ref=nres.at[i], dst_ref=resid_ref.at[0, :, :, columns], send_sem=ress.at[i], recv_sem=resr,
            device_id=(lax.rem(j + 1, 32), i), device_id_type=MESH,
        )
        cp.start()
        res_copies.append(cp)

    r_me = 2 * y + lax.rem(q // 2, 4) // 2
    is_worker = q == 4 * lax.rem(r_me, 2) + 2 * lax.rem(y, 2)
    block = 8 * s + r_me
    group = lane // 32

    def send_back(j_at, state, base):
        for c in range(2):
            parts = [state(c, base + 8 * g) for g in range(4)]
            for i in range(4):
                acc = pltpu.roll(parts[0], (128 - 32 * i) % 128, 1) if i else parts[0]
                for g in range(1, 4):
                    amount = (32 * (g - i)) % 128
                    part = pltpu.roll(parts[g], amount, 1) if amount else parts[g]
                    acc = jnp.where(group == g, part, acc)
                ret[4 * j_at + i, c, :, :] = acc
        for i in range(4):
            mine = (j_at + 1 == j) & (s == i)

            @pl.when(jnp.logical_not(mine))
            def _(i=i):
                pltpu.make_async_remote_copy(
                    src_ref=ret.at[4 * j_at + i], dst_ref=back.at[block], send_sem=rets, recv_sem=retr,
                    device_id=(j_at + 1, i), device_id_type=MESH,
                ).start()

            @pl.when(mine)
            def _(i=i):
                pltpu.make_async_copy(ret.at[4 * j_at + i], back.at[block], retr).start()

    def await_terms(j_at, h):
        view = got.at[j_at, :, pl.ds(HALO - h, B + 2 * h), :]
        pltpu.make_async_copy(view, view, gr.at[j_at]).wait()

    @pl.when(is_worker)
    def _():
        await_terms(0, 64)
        for c in range(2):
            s0[c, pl.ds(OFF, GW), :] = got[0, c, :GW, :]
        send_back(0, lambda c, o: s0[c, pl.ds(o, 8), :], OFF + HALO)

        def pair(j_first, h_first, h_second, n1, n2):
            for p, (src, dst, h) in enumerate(((s0, s1, h_first), (s1, s0, h_second))):
                at = j_first + p
                await_terms(at, h)
                begin = OFF + HALO - 2 * (30 - at)
                heun(
                    src, smid, dst, begin, n1, n2, masks, COARSE,
                    extra=lambda c, o, at=at: got[at, c, pl.ds(o - OFF, 8), :],
                )
                send_back(at, lambda c, o, dst=dst: dst[c, pl.ds(o, 8), :], OFF + HALO)

        at = 1
        while at < 30:
            h1, h2 = halo_of(at), halo_of(at + 1)
            end = at + 2
            while end < 30 and (halo_of(end), halo_of(end + 1)) == (h1, h2) and end - at < 4:
                end += 2
            width = B + 4 * (30 - at)
            n1, n2 = (width + 2 + 7) // 8, (width + 7) // 8
            if end - at > 2:

                def body(t, _, at=at, h1=h1, h2=h2, n1=n1, n2=n2):
                    pair(at + 2 * t, h1, h2, n1, n2)
                    return 0

                lax.fori_loop(0, (end - at) // 2, body, 0)
            else:
                pair(at, h1, h2, n1, n2)
            at = end

    @pl.when(j == 0)
    def _():
        for c in range(2):
            for t in range(2):
                turned = (abuf[c, pl.ds(OFF + 64 + 128 * t, 128), :] * (1.0 / SCALE)).T
                for i in range(4):
                    win[i, c, :, 128 * t : 128 * t + 128] = turned[32 * i : 32 * i + 32, :]
        coarse_ref[0, :, :, columns] = win[s, :, :, :256]
        copies = []
        for d in (1, 2, 3):
            to = lax.rem(s + d, 4)
            cp = pltpu.make_async_remote_copy(
                src_ref=win.at[to, :, :, pl.ds(0, 256)], dst_ref=coarse_ref.at[0, :, :, columns],
                send_sem=row0s.at[d - 1], recv_sem=row0r.at[d - 1], device_id=(j, to), device_id_type=MESH,
            )
            cp.start()
            copies.append(cp)
        for cp in copies:
            cp.wait()

    @pl.when(j > 0)
    def _():
        pltpu.make_async_copy(back, back, retr).wait()
        for c in range(2):
            for half in range(2):
                strips = []
                for e in range(4):
                    packed = [back[16 * half + 4 * k + e, c, :, :] for k in range(4)]
                    for g in range(4):
                        acc = None
                        for k in range(4):
                            amount = (32 * (k - g)) % 128
                            part = pltpu.roll(packed[k], amount, 1) if amount else packed[k]
                            acc = part if acc is None else jnp.where(group == k, part, acc)
                        strips.append(acc)
                square = (jnp.concatenate(strips, axis=0) * (1.0 / SCALE)).T
                for k in range(4):
                    tile = 4 * half + k
                    coarse_ref[0, c, :, 128 * tile : 128 * tile + 128] = square[32 * k : 32 * k + 32, :]

    pltpu.make_async_copy(resid_ref, resid_ref, resr).wait()
    for cp in res_copies:
        cp.wait_send()

    def finish(copy, remote):
        if remote:
            copy.wait_send()

    gather(finish)

    @pl.when(is_worker & (j > 0))
    def _():
        view = ret.at[pl.ds(0, 123)]
        pltpu.make_async_copy(view, view, rets).wait()

    @pl.when(is_worker & (j == 0))
    def _():
        pltpu.make_async_copy(ret, ret, rets).wait()


def on_device(iterate):
    vmem = pl.BlockSpec(memory_space=pltpu.VMEM)
    dma = pltpu.SemaphoreType.DMA
    shape = jax.ShapeDtypeStruct((1, 2, 32, 1024), F32)
    return pl.pallas_call(
        kernel,
        out_shape=(shape, shape),
        in_specs=[vmem],
        out_specs=(vmem, vmem),
        scratch_shapes=[
            pltpu.VMEM((2, 32, 1152), F32),
            pltpu.VMEM((4, 2, 32, WINDOW), F32),
            pltpu.VMEM((2, ROWS, 128), F32),
            pltpu.VMEM((2, ROWS, 128), F32),
            pltpu.VMEM((2, ROWS, 128), F32),
            pltpu.VMEM((2, ROWS, 128), F32),
            pltpu.VMEM((2, 256, 128), F32),
            pltpu.VMEM((2, 256, 128), F32),
            pltpu.VMEM((2, 256, 128), F32),
            pltpu.VMEM((31, 2, GW + 16, 128), F32),
            pltpu.VMEM((2, GW + 32, 128), F32),
            pltpu.VMEM((2, GW + 32, 128), F32),
            pltpu.VMEM((2, GW + 32, 128), F32),
            pltpu.VMEM((124, 2, 8, 128), F32),
            pltpu.VMEM((32, 2, 8, 128), F32),
            pltpu.VMEM((4, 2, 32, 256), F32),
            dma((3,)), dma((3,)),
            pltpu.SemaphoreType.REGULAR,
            dma, dma,
            dma((12,)), dma((31,)),
            dma, dma,
            dma((4,)), dma,
            dma((3,)), dma((3,)),
        ],
        compiler_params=pltpu.CompilerParams(
            collective_id=0, has_side_effects=True, vmem_limit_bytes=48 * 2**20
        ),
    )(iterate)


def solution(mesh):
    spec = P("tm", None, "space", None)
    return jax.shard_map(on_device, mesh=mesh, in_specs=(spec,), out_specs=(spec, spec), check_vma=False)
```

```python
import jax
import jax.numpy as jnp
from jax import lax
from jax.experimental import pallas as pl
from jax.experimental.pallas import tpu as pltpu
from jax.sharding import PartitionSpec as P

MESH = pl.DeviceIdType.MESH
F32 = jnp.float32
H = 0.015625
SCALE = H / 2
VISC = 0.8
FINE = (1.0 - 4.0 * VISC * H, VISC * H, 1.0)
COARSE = (1.0 - 64.0 * VISC * H, 16.0 * VISC * H, 16.0)
WINDOW = 384
OFF = 8
ROWS = 432
B = 32
HALO = 32
STEPS = 15
BATCHES = (5, 10, 13, 15)
GW = B + 2 * HALO


def stage(src, o, masks, consts):
    c0, k, q = consts
    u = src[0, pl.ds(o, 8), :]
    v = src[1, pl.ds(o, 8), :]
    su, sv = (u, v) if q == 1.0 else (q * u, q * v)
    a, b = k - su, k + su
    c = jnp.where(masks[0], k - sv, 0.0)
    d = jnp.where(masks[1], k + sv, 0.0)
    out = []
    for i, x in ((0, u), (1, v)):
        east = src[i, pl.ds(o + 1, 8), :]
        west = src[i, pl.ds(o - 1, 8), :]
        north = pltpu.roll(x, 127, 1)
        south = pltpu.roll(x, 1, 1)
        out.append((c0 * x + a * east) + (b * west + c * north) + d * south)
    return out


def heun(src, mid, dst, start, n1, n2, masks, consts, dst_shift=0, extra=None):
    for i in range(n1):
        o = start - 1 + 8 * i
        m = stage(src, o, masks, consts)
        for c in range(2):
            mid[c, pl.ds(o, 8), :] = m[c]
    for i in range(n2):
        o = start + 8 * i
        m = stage(mid, o, masks, consts)
        for c in range(2):
            new = 0.5 * (src[c, pl.ds(o, 8), :] + m[c])
            if extra is not None:
                new = new + extra(c, o)
            dst[c, pl.ds(o + dst_shift, 8), :] = new


def fine_steps(first, count, even, odd, mid, masks):
    for g in range(first, first + count, 8):
        n1 = (WINDOW - 2 - 4 * g + 7) // 8
        n2 = (WINDOW - 4 - 4 * g + 7) // 8

        def body(t, _):
            for p, (src, dst) in enumerate(((even, odd), (odd, even))):
                start = OFF + 2 * (2 * t + p) + 2
                heun(src, mid, dst, start, n1, n2, masks, FINE)
            return 0

        lax.fori_loop(g // 2, g // 2 + 4, body, 0)


def halo_of(slot):
    return 8 * ((2 * (STEPS - slot) + 7) // 8)


def slot_classes():
    edges = [n for n in range(STEPS + 1) if n == 0 or halo_of(n) != halo_of(n - 1)]
    return [(n, m, halo_of(n)) for n, m in zip(edges, edges[1:] + [STEPS + 1])]


def chain_tm(half, r):
    y = r // 4 + half * (3 - 2 * (r // 4))
    z = r // 4 * (7 - 2 * r) + r
    return 8 * y + 2 * z


def kernel(
    x_ref, coarse_ref, resid_ref,
    xbuf, rot, win, abuf, bbuf, dbuf, mid, cbuf, terms, relin, got, s0, s1, smid, ret, back, nres,
    xin, xs, xr, ysem, rels, relr, gs, gr, hs, rets, retr, ress, resr, row0s, row0r,
):
    j = lax.axis_index("tm")
    s = lax.axis_index("space")
    y, q = j // 8, lax.rem(j, 8)
    lane = lax.broadcasted_iota(jnp.int32, (8, 128), 1)
    masks = (lane < 127, lane > 0)

    fetch = pltpu.make_async_copy(x_ref.at[0], xbuf, xin)
    fetch.start()
    barrier = pltpu.get_barrier_semaphore()
    ring_x = [(j, lax.rem(s + d, 4)) for d in (1, 2, 3)]
    ring_y = [(lax.rem(y + d, 4) * 8 + q, s) for d in (1, 2, 3)]
    plane = [(y * 8 + lax.rem(q + d, 8), s) for d in range(1, 8)]
    for other in ring_x + ring_y + plane:
        pl.semaphore_signal(barrier, inc=1, device_id=other, device_id_type=MESH)
    fetch.wait()

    low = lax.broadcasted_iota(jnp.int32, (32, 128), 1) < 64
    for c in range(2):
        turned = [pltpu.roll(xbuf[c, :, 128 * t : 128 * t + 128], 64, 1) for t in range(8)]
        for t in range(9):
            rot[c, :, 128 * t : 128 * t + 128] = jnp.where(low, turned[(t - 1) % 8], turned[t % 8])

    pl.semaphore_wait(barrier, 13)

    sends = []
    for d in (1, 2, 3):
        to = lax.rem(s + d, 4)
        cp = pltpu.make_async_remote_copy(
            src_ref=rot.at[:, :, pl.ds(pl.multiple_of(256 * to, 128), WINDOW)],
            dst_ref=win.at[s],
            send_sem=xs.at[d - 1],
            recv_sem=xr.at[d - 1],
            device_id=(j, to),
            device_id_type=MESH,
        )
        cp.start()
        sends.append(cp)
    win[s] = rot[:, :, pl.ds(pl.multiple_of(256 * s, 128), WINDOW)]
    for cp in sends:
        cp.wait()
    for other in ring_y:
        pl.semaphore_signal(ysem, inc=1, device_id=other, device_id_type=MESH)
    for c in range(2):
        for t in range(3):
            tile = jnp.concatenate([win[i, c, :, 128 * t : 128 * t + 128] for i in range(4)], axis=0)
            abuf[c, OFF + 128 * t : OFF + 128 * t + 128, :] = tile.T * SCALE

    fine_steps(0, 16, abuf, bbuf, mid, masks)

    pl.semaphore_wait(ysem, 3)
    own = pl.ds(OFF + 64, 256)
    before = pltpu.make_async_remote_copy(
        src_ref=abuf.at[:, own, :], dst_ref=relin, send_sem=rels, recv_sem=relr,
        device_id=(lax.rem(j + 31, 32), s), device_id_type=MESH,
    )
    before.start()

    heun(abuf, mid, cbuf, OFF + 64, 33, 32, masks, COARSE, dst_shift=-(OFF + 64))
    for c in range(2):
        dbuf[c, :, :] = abuf[c, :, :]
    fine_steps(16, 16, dbuf, bbuf, mid, masks)

    for i in range(32):
        for c in range(2):
            rows = pl.ds(8 * i, 8)
            coarse = jnp.where(j > 0, cbuf[c, rows, :], 0.0)
            terms[c, rows, :] = dbuf[c, pl.ds(OFF + 64 + 8 * i, 8), :] - coarse

    half = j // 16
    slot = j - STEPS * half

    def gather(act):
        for first, end, h in slot_classes():

            def pieces(h=h):
                for r in range(-1, 9):
                    lo, hi = max(0, B * r - h), min(256, B * r + B + h)
                    if hi <= lo:
                        continue
                    src = terms.at[:, pl.ds(lo, hi - lo), :]
                    dst = got.at[slot, :, pl.ds(lo - (B * r - HALO), hi - lo), :]
                    holder = chain_tm(half, r % 8)
                    to = lax.rem(s + (r // 8) + 4, 4)

                    def remote(src=src, dst=dst, r=r, holder=holder, to=to):
                        act(
                            pltpu.make_async_remote_copy(
                                src_ref=src, dst_ref=dst, send_sem=gs.at[r + 1], recv_sem=gr.at[slot],
                                device_id=(holder, to), device_id_type=MESH,
                            ),
                            True,
                        )

                    if 0 <= r < 8:
                        pl.when(j != holder)(remote)

                        @pl.when(j == holder)
                        def _(src=src, dst=dst):
                            act(pltpu.make_async_copy(src, dst, gr.at[slot]), False)
                    else:
                        remote()

            pl.when((slot >= first) & (slot < end))(pieces)

    def start(copy, remote):
        copy.start()

    gather(start)

    before.wait()
    is_worker = lax.rem(j, 2) == 0
    columns = pl.ds(pl.multiple_of(256 * s, 128), 256)

    def residual():
        for c in range(2):
            for t in range(2):
                rows = pl.ds(OFF + 64 + 128 * t, 128)
                diff = dbuf[c, rows, :] - relin[c, 128 * t : 128 * t + 128, :]
                diff = jnp.where(j < 31, diff, 0.0).T
                for i in range(4):
                    nres[i, c, :, 128 * t : 128 * t + 128] = diff[32 * i : 32 * i + 32, :]
        for i in range(4):
            res_copy(i).start()

    def res_copy(i):
        return pltpu.make_async_remote_copy(
            src_ref=nres.at[i], dst_ref=resid_ref.at[0, :, :, columns], send_sem=ress.at[i], recv_sem=resr,
            device_id=(lax.rem(j + 1, 32), i), device_id_type=MESH,
        )

    def finish(copy, remote):
        if remote:
            copy.wait_send()

    @pl.when(jnp.logical_not(is_worker))
    def _():
        gather(finish)

    @pl.when(jnp.logical_not(is_worker & (half == 0)))
    def _():
        residual()

    r_me = 4 * jnp.where(half == 0, y, 3 - y) + jnp.where((y == 0) | (y == 3), q // 2, 3 - q // 2)
    block = 8 * s + r_me
    group = lane // 32

    def pack(n, state, base):
        for c in range(2):
            parts = [state[c, base + 8 * g : base + 8 * g + 8, :] for g in range(4)]
            for i in range(4):
                acc = pltpu.roll(parts[0], (128 - 32 * i) % 128, 1) if i else parts[0]
                for g in range(1, 4):
                    amount = (32 * (g - i)) % 128
                    part = pltpu.roll(parts[g], amount, 1) if amount else parts[g]
                    acc = jnp.where(group == g, part, acc)
                ret[4 * n + i, c, :, :] = acc

    def send_back(n):
        row = STEPS * half + n + 1

        def remote(i):
            pltpu.make_async_remote_copy(
                src_ref=ret.at[4 * n + i], dst_ref=back.at[block], send_sem=rets, recv_sem=retr,
                device_id=(row, i), device_id_type=MESH,
            ).start()

        @pl.when(row != j)
        def _():
            for i in range(4):
                remote(i)

        @pl.when(row == j)
        def _():
            for i in range(4):

                @pl.when(s != i)
                def _(i=i):
                    remote(i)

                @pl.when(s == i)
                def _(i=i):
                    pltpu.make_async_copy(ret.at[4 * n + i], back.at[block], retr).start()

    def send_back_from(first, end):
        def body(n, _):
            send_back(n)
            return 0

        lax.fori_loop(first, end, body, 0)

    def await_terms(n):
        view = got.at[n, :, pl.ds(HALO - halo_of(n), B + 2 * halo_of(n)), :]
        pltpu.make_async_copy(view, view, gr.at[n]).wait()

    def hand_over(d):
        r = r_me + d + 8
        return pltpu.make_async_remote_copy(
            src_ref=s1.at[:, pl.ds(OFF + HALO, B), :], dst_ref=got.at[0, :, pl.ds(HALO - B * d, B), :],
            send_sem=hs.at[d + 1], recv_sem=gr.at[0],
            device_id=(chain_tm(1, lax.rem(r, 8)), lax.rem(s + r // 8 + 3, 4)), device_id_type=MESH,
        )

    @pl.when(is_worker)
    def _():
        for n in range(STEPS + 1):
            await_terms(n)
        for c in range(2):
            s0[c, pl.ds(OFF, GW), :] = got[0, c, :GW, :]
        pack(0, s0, OFF + HALO)
        for n in range(1, STEPS + 1):
            src, dst = (s0, s1) if n % 2 else (s1, s0)
            left = STEPS - n
            width = B + 4 * left
            heun(
                src, smid, dst, OFF + HALO - 2 * left, (width + 9) // 8, (width + 7) // 8, masks, COARSE,
                extra=lambda c, o, n=n: got[n, c, pl.ds(o - OFF, 8), :],
            )
            if n == STEPS:

                @pl.when(half == 0)
                def _():
                    for d in (-1, 0, 1):
                        hand_over(d).start()

            pack(n, dst, OFF + HALO)
            if n in BATCHES:
                first = max([m for m in BATCHES if m < n], default=0) + 1
                pl.when(half == 1)(lambda first=first, n=n: send_back_from(first, n + 1))

        pl.when(half == 0)(lambda: send_back_from(0, STEPS + 1))

    @pl.when(is_worker & (half == 0))
    def _():
        residual()

    @pl.when(j == 0)
    def _():
        for c in range(2):
            for t in range(2):
                turned = abuf[c, pl.ds(OFF + 64 + 128 * t, 128), :].T
                for i in range(4):
                    win[i, c, :, 128 * t : 128 * t + 128] = turned[32 * i : 32 * i + 32, :]
        coarse_ref[0, :, :, columns] = win[s, :, :, :256]
        copies = []
        for d in (1, 2, 3):
            to = lax.rem(s + d, 4)
            cp = pltpu.make_async_remote_copy(
                src_ref=win.at[to, :, :, pl.ds(0, 256)], dst_ref=coarse_ref.at[0, :, :, columns],
                send_sem=row0s.at[d - 1], recv_sem=row0r.at[d - 1], device_id=(j, to), device_id_type=MESH,
            )
            cp.start()
            copies.append(cp)
        for cp in copies:
            cp.wait()

    @pl.when(j > 0)
    def _():
        pltpu.make_async_copy(back, back, retr).wait()
        for c in range(2):
            for half in range(2):
                strips = []
                for e in range(4):
                    packed = [back[16 * half + 4 * k + e, c, :, :] for k in range(4)]
                    for g in range(4):
                        acc = None
                        for k in range(4):
                            amount = (32 * (k - g)) % 128
                            part = pltpu.roll(packed[k], amount, 1) if amount else packed[k]
                            acc = part if acc is None else jnp.where(group == k, part, acc)
                        strips.append(acc)
                square = jnp.concatenate(strips, axis=0).T
                for k in range(4):
                    tile = 4 * half + k
                    coarse_ref[0, c, :, 128 * tile : 128 * tile + 128] = square[32 * k : 32 * k + 32, :]

    pltpu.make_async_copy(resid_ref, resid_ref, resr).wait()
    for i in range(4):
        res_copy(i).wait_send()

    @pl.when(is_worker)
    def _():
        gather(finish)

    @pl.when(is_worker & (half == 0))
    def _():
        for d in (-1, 0, 1):
            hand_over(d).wait_send()

    for which, first, count in ((0, 0, 4 * STEPS + 4), (1, 4, 4 * STEPS)):

        @pl.when(is_worker & (half == which) & (lax.rem(j, 16) == 0))
        def _(first=first, count=count):
            view = ret.at[pl.ds(first, count)]
            pltpu.make_async_copy(view, view, rets).wait()

        @pl.when(is_worker & (half == which) & (lax.rem(j, 16) > 0))
        def _(first=first, count=count):
            view = ret.at[pl.ds(first, count - 1)]
            pltpu.make_async_copy(view, view, rets).wait()


def on_device(iterate):
    vmem = pl.BlockSpec(memory_space=pltpu.VMEM)
    dma = pltpu.SemaphoreType.DMA
    shape = jax.ShapeDtypeStruct((1, 2, 32, 1024), F32)
    coarse, resid = pl.pallas_call(
        kernel,
        out_shape=(shape, shape),
        in_specs=[pl.BlockSpec(memory_space=pl.ANY)],
        out_specs=(vmem, vmem),
        scratch_shapes=[
            pltpu.VMEM((2, 32, 1024), F32),
            pltpu.VMEM((2, 32, 1152), F32),
            pltpu.VMEM((4, 2, 32, WINDOW), F32),
            pltpu.VMEM((2, ROWS, 128), F32),
            pltpu.VMEM((2, ROWS, 128), F32),
            pltpu.VMEM((2, ROWS, 128), F32),
            pltpu.VMEM((2, ROWS, 128), F32),
            pltpu.VMEM((2, 256, 128), F32),
            pltpu.VMEM((2, 256, 128), F32),
            pltpu.VMEM((2, 256, 128), F32),
            pltpu.VMEM((STEPS + 1, 2, GW + 16, 128), F32),
            pltpu.VMEM((2, GW + 32, 128), F32),
            pltpu.VMEM((2, GW + 32, 128), F32),
            pltpu.VMEM((2, GW + 32, 128), F32),
            pltpu.VMEM((4 * STEPS + 4, 2, 8, 128), F32),
            pltpu.VMEM((32, 2, 8, 128), F32),
            pltpu.VMEM((4, 2, 32, 256), F32),
            dma, dma((3,)), dma((3,)),
            pltpu.SemaphoreType.REGULAR,
            dma, dma,
            dma((10,)), dma((STEPS + 1,)), dma((3,)),
            dma, dma,
            dma((4,)), dma,
            dma((3,)), dma((3,)),
        ],
        compiler_params=pltpu.CompilerParams(
            collective_id=0, has_side_effects=True, vmem_limit_bytes=48 * 2**20
        ),
    )(iterate)
    return coarse * (1.0 / SCALE), resid * (1.0 / SCALE)


def solution(mesh):
    spec = P("tm", None, "space", None)
    return jax.shard_map(on_device, mesh=mesh, in_specs=(spec,), out_specs=(spec, spec), check_vma=False)
```

```python
import jax
import jax.numpy as jnp
from jax import lax
from jax.experimental import pallas as pl
from jax.experimental.pallas import tpu as pltpu
from jax.sharding import PartitionSpec as P

MESH = pl.DeviceIdType.MESH
F32 = jnp.float32
H = 0.015625
SCALE = H / 2
VISC = 0.8
FINE = (1.0 - 4.0 * VISC * H, VISC * H, 1.0)
COARSE = (1.0 - 64.0 * VISC * H, 16.0 * VISC * H, 16.0)
WINDOW = 384
OFF = 8
ROWS = 432
B = 32
STEPS = (15, 15)
HALO = 8 * ((2 * max(STEPS) + 7) // 8)
BATCHES = tuple(sorted({max(STEPS) - d for d in (0, 2, 5, 10, 15) if max(STEPS) > d}))
GW = B + 2 * HALO


def stage(src, o, masks, consts):
    c0, k, q = consts
    u = src[0, pl.ds(o, 8), :]
    v = src[1, pl.ds(o, 8), :]
    su, sv = (u, v) if q == 1.0 else (q * u, q * v)
    a, b = k - su, k + su
    c = jnp.where(masks[0], k - sv, 0.0)
    d = jnp.where(masks[1], k + sv, 0.0)
    out = []
    for i, x in ((0, u), (1, v)):
        east = src[i, pl.ds(o + 1, 8), :]
        west = src[i, pl.ds(o - 1, 8), :]
        north = pltpu.roll(x, 127, 1)
        south = pltpu.roll(x, 1, 1)
        out.append((c0 * x + a * east) + (b * west + c * north) + d * south)
    return out


def heun(src, mid, dst, start, n1, n2, masks, consts, dst_shift=0, extra=None):
    for i in range(n1):
        o = start - 1 + 8 * i
        m = stage(src, o, masks, consts)
        for c in range(2):
            mid[c, pl.ds(o, 8), :] = m[c]
    for i in range(n2):
        o = start + 8 * i
        m = stage(mid, o, masks, consts)
        for c in range(2):
            new = 0.5 * (src[c, pl.ds(o, 8), :] + m[c])
            if extra is not None:
                new = new + extra(c, o)
            dst[c, pl.ds(o + dst_shift, 8), :] = new


def fine_steps(first, count, even, odd, mid, masks):
    for g in range(first, first + count, 4):
        n1 = (WINDOW - 2 - 4 * g + 7) // 8
        n2 = (WINDOW - 4 - 4 * g + 7) // 8

        def body(t, _):
            for p, (src, dst) in enumerate(((even, odd), (odd, even))):
                start = OFF + 2 * (2 * t + p) + 2
                heun(src, mid, dst, start, n1, n2, masks, FINE)
            return 0

        lax.fori_loop(g // 2, g // 2 + 2, body, 0)


def halo_of(part, slot):
    return 4 * ((2 * (STEPS[part] - slot) + 3) // 4)


def slot_classes(part):
    slots = range(part, STEPS[part] + 1)
    edges = [n for n in slots if n == part or halo_of(part, n) != halo_of(part, n - 1)]
    return [(n, m, halo_of(part, n)) for n, m in zip(edges, edges[1:] + [STEPS[part] + 1])]


WORKERS = (
    (0, 2, 4, 6, 14, 12, 10, 8),
    (25, 27, 29, 31, 23, 21, 19, 17),
)


def pick(table, r):
    return sum(jnp.where(r == i, tm, 0) for i, tm in enumerate(table))


def kernel(
    x_ref, coarse_ref, resid_ref,
    xbuf, rot, win, abuf, bbuf, dbuf, mid, cbuf, terms, relin, got, s0, s1, smid, ret, back, nres,
    xin, xs, xr, ysem, rels, relr, gs, gr, hs, rets, retr, ress, resr, row0s, row0r,
):
    j = lax.axis_index("tm")
    s = lax.axis_index("space")
    y, q = j // 8, lax.rem(j, 8)
    lane = lax.broadcasted_iota(jnp.int32, (8, 128), 1)
    masks = (lane < 127, lane > 0)

    fetch = pltpu.make_async_copy(x_ref.at[0], xbuf, xin)
    fetch.start()
    barrier = pltpu.get_barrier_semaphore()
    ring_x = [(j, lax.rem(s + d, 4)) for d in (1, 2, 3)]
    ring_y = [(lax.rem(y + d, 4) * 8 + q, s) for d in (1, 2, 3)]
    plane = [(y * 8 + lax.rem(q + d, 8), s) for d in range(1, 8)]
    for other in ring_x + ring_y + plane:
        pl.semaphore_signal(barrier, inc=1, device_id=other, device_id_type=MESH)
    fetch.wait()

    low = lax.broadcasted_iota(jnp.int32, (32, 128), 1) < 64
    for c in range(2):
        turned = [pltpu.roll(xbuf[c, :, 128 * t : 128 * t + 128], 64, 1) for t in range(8)]
        for t in range(9):
            rot[c, :, 128 * t : 128 * t + 128] = jnp.where(low, turned[(t - 1) % 8], turned[t % 8])

    pl.semaphore_wait(barrier, 13)

    sends = []
    for d in (1, 2, 3):
        to = lax.rem(s + d, 4)
        cp = pltpu.make_async_remote_copy(
            src_ref=rot.at[:, :, pl.ds(pl.multiple_of(256 * to, 128), WINDOW)],
            dst_ref=win.at[s],
            send_sem=xs.at[d - 1],
            recv_sem=xr.at[d - 1],
            device_id=(j, to),
            device_id_type=MESH,
        )
        cp.start()
        sends.append(cp)
    win[s] = rot[:, :, pl.ds(pl.multiple_of(256 * s, 128), WINDOW)]
    for cp in sends:
        cp.wait()
    for other in ring_y:
        pl.semaphore_signal(ysem, inc=1, device_id=other, device_id_type=MESH)
    for c in range(2):
        for t in range(3):
            tile = jnp.concatenate([win[i, c, :, 128 * t : 128 * t + 128] for i in range(4)], axis=0)
            abuf[c, OFF + 128 * t : OFF + 128 * t + 128, :] = tile.T * SCALE

    fine_steps(0, 16, abuf, bbuf, mid, masks)

    pl.semaphore_wait(ysem, 3)
    own = pl.ds(OFF + 64, 256)
    before = pltpu.make_async_remote_copy(
        src_ref=abuf.at[:, own, :], dst_ref=relin, send_sem=rels, recv_sem=relr,
        device_id=(lax.rem(j + 31, 32), s), device_id_type=MESH,
    )
    before.start()

    heun(abuf, mid, cbuf, OFF + 64, 33, 32, masks, COARSE, dst_shift=-(OFF + 64))
    for c in range(2):
        dbuf[c, :, :] = abuf[c, :, :]
    fine_steps(16, 16, dbuf, bbuf, mid, masks)

    for i in range(32):
        for c in range(2):
            rows = pl.ds(8 * i, 8)
            coarse = jnp.where(j > 0, cbuf[c, rows, :], 0.0)
            terms[c, rows, :] = dbuf[c, pl.ds(OFF + 64 + 8 * i, 8), :] - coarse

    def gather(act):
        for part in range(2):
            slot = j - STEPS[0] * part
            for first, end, h in slot_classes(part):

                def pieces(part=part, slot=slot, h=h):
                    for r in range(-2, 10):
                        lo, hi = max(0, B * r - h), min(256, B * r + B + h)
                        if hi <= lo:
                            continue
                        src = terms.at[:, pl.ds(lo, hi - lo), :]
                        dst = got.at[slot, :, pl.ds(lo - (B * r - HALO), hi - lo), :]
                        holder = WORKERS[part][r % 8]
                        to = lax.rem(s + (r // 8) + 4, 4)

                        def remote(src=src, dst=dst, r=r, holder=holder, to=to):
                            act(
                                pltpu.make_async_remote_copy(
                                    src_ref=src, dst_ref=dst, send_sem=gs.at[r + 2], recv_sem=gr.at[slot],
                                    device_id=(holder, to), device_id_type=MESH,
                                ),
                                True,
                            )

                        if 0 <= r < 8:
                            pl.when(j != holder)(remote)

                            @pl.when(j == holder)
                            def _(src=src, dst=dst):
                                act(pltpu.make_async_copy(src, dst, gr.at[slot]), False)
                        else:
                            remote()

                pl.when((slot >= first) & (slot < end))(pieces)

    def start(copy, remote):
        copy.start()

    gather(start)

    before.wait()
    half = sum(jnp.where(j == tm, 1, 0) for tm in WORKERS[1])
    is_worker = sum(jnp.where(j == tm, 1, 0) for tm in WORKERS[0] + WORKERS[1]) > 0
    columns = pl.ds(pl.multiple_of(256 * s, 128), 256)

    def residual():
        for c in range(2):
            for t in range(2):
                rows = pl.ds(OFF + 64 + 128 * t, 128)
                diff = dbuf[c, rows, :] - relin[c, 128 * t : 128 * t + 128, :]
                diff = jnp.where(j < 31, diff, 0.0).T
                for i in range(4):
                    nres[i, c, :, 128 * t : 128 * t + 128] = diff[32 * i : 32 * i + 32, :]
        for i in range(4):
            res_copy(i).start()

    def res_copy(i):
        return pltpu.make_async_remote_copy(
            src_ref=nres.at[i], dst_ref=resid_ref.at[0, :, :, columns], send_sem=ress.at[i], recv_sem=resr,
            device_id=(lax.rem(j + 1, 32), i), device_id_type=MESH,
        )

    def finish(copy, remote):
        if remote:
            copy.wait_send()

    @pl.when(jnp.logical_not(is_worker))
    def _():
        gather(finish)

    @pl.when(jnp.logical_not(is_worker & (half == 0)))
    def _():
        residual()

    r_me = sum(jnp.where(j == tm, r, 0) for table in WORKERS for r, tm in enumerate(table))
    block = 8 * s + r_me
    group = lane // 32

    def pack(n, state, base):
        for c in range(2):
            parts = [state[c, base + 8 * g : base + 8 * g + 8, :] for g in range(4)]
            for i in range(4):
                acc = pltpu.roll(parts[0], (128 - 32 * i) % 128, 1) if i else parts[0]
                for g in range(1, 4):
                    amount = (32 * (g - i)) % 128
                    part = pltpu.roll(parts[g], amount, 1) if amount else parts[g]
                    acc = jnp.where(group == g, part, acc)
                ret[4 * n + i, c, :, :] = acc

    def send_back(part, n):
        row = STEPS[0] * part + n + 1

        def remote(i):
            pltpu.make_async_remote_copy(
                src_ref=ret.at[4 * n + i], dst_ref=back.at[block], send_sem=rets, recv_sem=retr,
                device_id=(row, i), device_id_type=MESH,
            ).start()

        @pl.when(row != j)
        def _():
            for i in range(4):
                remote(i)

        @pl.when(row == j)
        def _():
            for i in range(4):

                @pl.when(s != i)
                def _(i=i):
                    remote(i)

                @pl.when(s == i)
                def _(i=i):
                    pltpu.make_async_copy(ret.at[4 * n + i], back.at[block], retr).start()

    def send_back_from(part, first, end):
        def body(n, _):
            send_back(part, n)
            return 0

        lax.fori_loop(first, end, body, 0)

    def await_terms(part, n):
        h = halo_of(part, n)
        view = got.at[n, :, pl.ds(HALO - h, B + 2 * h), :]
        pltpu.make_async_copy(view, view, gr.at[n]).wait()

    last_state = s1 if STEPS[0] % 2 else s0
    first_h = halo_of(1, 0)

    def hand_over(d):
        lo, hi = max(0, B * d - first_h), min(B, B * d + B + first_h)
        r = r_me + d + 8
        return pltpu.make_async_remote_copy(
            src_ref=last_state.at[:, pl.ds(OFF + HALO + lo, hi - lo), :],
            dst_ref=got.at[0, :, pl.ds(HALO - B * d + lo, hi - lo), :],
            send_sem=hs.at[d + 2], recv_sem=gr.at[0],
            device_id=(pick(WORKERS[1], lax.rem(r, 8)), lax.rem(s + r // 8 + 3, 4)), device_id_type=MESH,
        )

    near = [d for d in (-2, -1, 0, 1, 2) if abs(d) * B < B + first_h]

    def chain(part):
        for n in range(STEPS[part] + 1):
            await_terms(part, n)
        for c in range(2):
            s0[c, pl.ds(OFF, GW), :] = got[0, c, :GW, :]
        if part == 0:
            pack(0, s0, OFF + HALO)
        for n in range(1, STEPS[part] + 1):
            src, dst = (s0, s1) if n % 2 else (s1, s0)
            left = STEPS[part] - n
            width = B + 4 * left
            heun(
                src, smid, dst, OFF + HALO - 2 * left, (width + 9) // 8, (width + 7) // 8, masks, COARSE,
                extra=lambda c, o, n=n: got[n, c, pl.ds(o - OFF, 8), :],
            )
            if part == 0 and n == STEPS[0]:
                for d in near:
                    hand_over(d).start()
            pack(n, dst, OFF + HALO)
            if part == 1 and n in BATCHES:
                send_back_from(1, max([m for m in BATCHES if m < n], default=0) + 1, n + 1)
        if part == 0:
            send_back_from(0, 0, STEPS[0] + 1)

    for which in range(2):
        pl.when(is_worker & (half == which))(lambda which=which: chain(which))

    @pl.when(is_worker & (half == 0))
    def _():
        residual()

    pltpu.make_async_copy(resid_ref, resid_ref, resr).wait()
    for i in range(4):
        res_copy(i).wait_send()

    @pl.when(is_worker)
    def _():
        gather(finish)

    @pl.when(is_worker & (half == 0))
    def _():
        for d in near:
            hand_over(d).wait_send()

    for which, first, count in ((0, 0, 4 * STEPS[0] + 4), (1, 4, 4 * STEPS[1])):
        inside = (j > 0) & (j < STEPS[0] + 2) if which == 0 else j > STEPS[0] + 1

        @pl.when(is_worker & (half == which) & inside)
        def _(first=first, count=count):
            view = ret.at[pl.ds(first, count - 1)]
            pltpu.make_async_copy(view, view, rets).wait()

        @pl.when(is_worker & (half == which) & jnp.logical_not(inside))
        def _(first=first, count=count):
            view = ret.at[pl.ds(first, count)]
            pltpu.make_async_copy(view, view, rets).wait()

    @pl.when(j == 0)
    def _():
        for c in range(2):
            for t in range(2):
                turned = abuf[c, pl.ds(OFF + 64 + 128 * t, 128), :].T
                for i in range(4):
                    win[i, c, :, 128 * t : 128 * t + 128] = turned[32 * i : 32 * i + 32, :]
        coarse_ref[0, :, :, columns] = win[s, :, :, :256]
        copies = []
        for d in (1, 2, 3):
            to = lax.rem(s + d, 4)
            cp = pltpu.make_async_remote_copy(
                src_ref=win.at[to, :, :, pl.ds(0, 256)], dst_ref=coarse_ref.at[0, :, :, columns],
                send_sem=row0s.at[d - 1], recv_sem=row0r.at[d - 1], device_id=(j, to), device_id_type=MESH,
            )
            cp.start()
            copies.append(cp)
        for cp in copies:
            cp.wait()

    @pl.when(j > 0)
    def _():
        pltpu.make_async_copy(back, back, retr).wait()
        for c in range(2):
            for half in range(2):
                strips = []
                for e in range(4):
                    packed = [back[16 * half + 4 * k + e, c, :, :] for k in range(4)]
                    for g in range(4):
                        acc = None
                        for k in range(4):
                            amount = (32 * (k - g)) % 128
                            part = pltpu.roll(packed[k], amount, 1) if amount else packed[k]
                            acc = part if acc is None else jnp.where(group == k, part, acc)
                        strips.append(acc)
                square = jnp.concatenate(strips, axis=0).T
                for k in range(4):
                    tile = 4 * half + k
                    coarse_ref[0, c, :, 128 * tile : 128 * tile + 128] = square[32 * k : 32 * k + 32, :]


def on_device(iterate):
    vmem = pl.BlockSpec(memory_space=pltpu.VMEM)
    dma = pltpu.SemaphoreType.DMA
    shape = jax.ShapeDtypeStruct((1, 2, 32, 1024), F32)
    coarse, resid = pl.pallas_call(
        kernel,
        out_shape=(shape, shape),
        in_specs=[pl.BlockSpec(memory_space=pl.ANY)],
        out_specs=(vmem, vmem),
        scratch_shapes=[
            pltpu.VMEM((2, 32, 1024), F32),
            pltpu.VMEM((2, 32, 1152), F32),
            pltpu.VMEM((4, 2, 32, WINDOW), F32),
            pltpu.VMEM((2, ROWS, 128), F32),
            pltpu.VMEM((2, ROWS, 128), F32),
            pltpu.VMEM((2, ROWS, 128), F32),
            pltpu.VMEM((2, ROWS, 128), F32),
            pltpu.VMEM((2, 256, 128), F32),
            pltpu.VMEM((2, 256, 128), F32),
            pltpu.VMEM((2, 256, 128), F32),
            pltpu.VMEM((max(STEPS) + 1, 2, GW + 16, 128), F32),
            pltpu.VMEM((2, GW + 32, 128), F32),
            pltpu.VMEM((2, GW + 32, 128), F32),
            pltpu.VMEM((2, GW + 32, 128), F32),
            pltpu.VMEM((4 * max(STEPS) + 4, 2, 8, 128), F32),
            pltpu.VMEM((32, 2, 8, 128), F32),
            pltpu.VMEM((4, 2, 32, 256), F32),
            dma, dma((3,)), dma((3,)),
            pltpu.SemaphoreType.REGULAR,
            dma, dma,
            dma((12,)), dma((max(STEPS) + 1,)), dma((5,)),
            dma, dma,
            dma((4,)), dma,
            dma((3,)), dma((3,)),
        ],
        compiler_params=pltpu.CompilerParams(
            collective_id=0, has_side_effects=True, vmem_limit_bytes=48 * 2**20
        ),
    )(iterate)
    return coarse * (1.0 / SCALE), resid * (1.0 / SCALE)


def solution(mesh):
    spec = P("tm", None, "space", None)
    return jax.shard_map(on_device, mesh=mesh, in_specs=(spec,), out_specs=(spec, spec), check_vma=False)
```

```python
import jax
import jax.numpy as jnp
from jax import lax
from jax.experimental import pallas as pl
from jax.experimental.pallas import tpu as pltpu
from jax.sharding import PartitionSpec as P

MESH = pl.DeviceIdType.MESH
F32 = jnp.float32
H = 0.015625
SCALE = H / 2
VISC = 0.8
FINE = (1.0 - 4.0 * VISC * H, VISC * H, 1.0)
COARSE = (1.0 - 64.0 * VISC * H, 16.0 * VISC * H, 16.0)
WINDOW = 384
OFF = 8
ROWS = 432
B = 32
STEPS = (15, 15)
HALO = 8 * ((2 * max(STEPS) + 7) // 8)
BATCHES = tuple(sorted({max(STEPS) - d for d in (0, 2, 5, 10, 15) if max(STEPS) > d}))
GW = B + 2 * HALO


def stage(src, o, masks, consts):
    c0, k, q = consts
    u = src[0, pl.ds(o, 8), :]
    v = src[1, pl.ds(o, 8), :]
    su, sv = (u, v) if q == 1.0 else (q * u, q * v)
    a, b = k - su, k + su
    c = jnp.where(masks[0], k - sv, 0.0)
    d = jnp.where(masks[1], k + sv, 0.0)
    out = []
    for i, x in ((0, u), (1, v)):
        east = src[i, pl.ds(o + 1, 8), :]
        west = src[i, pl.ds(o - 1, 8), :]
        north = pltpu.roll(x, 127, 1)
        south = pltpu.roll(x, 1, 1)
        out.append((c0 * x + a * east) + (b * west + c * north) + d * south)
    return out


def heun(src, mid, dst, start, n1, n2, masks, consts, dst_shift=0, extra=None):
    for i in range(n1):
        o = start - 1 + 8 * i
        m = stage(src, o, masks, consts)
        for c in range(2):
            mid[c, pl.ds(o, 8), :] = m[c]
    for i in range(n2):
        o = start + 8 * i
        m = stage(mid, o, masks, consts)
        for c in range(2):
            new = 0.5 * (src[c, pl.ds(o, 8), :] + m[c])
            if extra is not None:
                new = new + extra(c, o)
            dst[c, pl.ds(o + dst_shift, 8), :] = new


def fine_steps(first, count, even, odd, mid, masks):
    for g in range(first, first + count, 4):
        n1 = (WINDOW - 2 - 4 * g + 7) // 8
        n2 = (WINDOW - 4 - 4 * g + 7) // 8

        def body(t, _):
            for p, (src, dst) in enumerate(((even, odd), (odd, even))):
                start = OFF + 2 * (2 * t + p) + 2
                heun(src, mid, dst, start, n1, n2, masks, FINE)
            return 0

        lax.fori_loop(g // 2, g // 2 + 2, body, 0)


def halo_of(part, slot):
    return 4 * ((2 * (STEPS[part] - slot) + 3) // 4)


def slot_classes(part):
    slots = range(part, STEPS[part] + 1)
    edges = [n for n in slots if n == part or halo_of(part, n) != halo_of(part, n - 1)]
    return [(n, m, halo_of(part, n)) for n, m in zip(edges, edges[1:] + [STEPS[part] + 1])]


WORKERS = (
    (0, 2, 4, 6, 14, 12, 10, 8),
    (25, 27, 29, 31, 23, 21, 19, 17),
)


def pick(table, r):
    return sum(jnp.where(r == i, tm, 0) for i, tm in enumerate(table))


def kernel(
    x_ref, coarse_ref, resid_ref,
    xbuf, rot, win, abuf, bbuf, dbuf, mid, cbuf, terms, relin, got, s0, s1, smid, ret, back, nres,
    xin, xs, xr, ysem, rels, relr, gs, gr, hs, rets, retr, ress, resr, row0s, row0r,
):
    j = lax.axis_index("tm")
    s = lax.axis_index("space")
    y, q = j // 8, lax.rem(j, 8)
    lane = lax.broadcasted_iota(jnp.int32, (8, 128), 1)
    masks = (lane < 127, lane > 0)

    fetch = pltpu.make_async_copy(x_ref.at[0], xbuf, xin)
    fetch.start()
    barrier = pltpu.get_barrier_semaphore()
    ring_x = [(j, lax.rem(s + d, 4)) for d in (1, 2, 3)]
    ring_y = [(lax.rem(y + d, 4) * 8 + q, s) for d in (1, 2, 3)]
    plane = [(y * 8 + lax.rem(q + d, 8), s) for d in range(1, 8)]
    for other in ring_x + ring_y + plane:
        pl.semaphore_signal(barrier, inc=1, device_id=other, device_id_type=MESH)
    fetch.wait()

    low = lax.broadcasted_iota(jnp.int32, (32, 128), 1) < 64
    for c in range(2):
        turned = [pltpu.roll(xbuf[c, :, 128 * t : 128 * t + 128], 64, 1) for t in range(8)]
        for t in range(9):
            rot[c, :, 128 * t : 128 * t + 128] = jnp.where(low, turned[(t - 1) % 8], turned[t % 8])

    pl.semaphore_wait(barrier, 13)

    sends = []
    for d in (1, 2, 3):
        to = lax.rem(s + d, 4)
        cp = pltpu.make_async_remote_copy(
            src_ref=rot.at[:, :, pl.ds(pl.multiple_of(256 * to, 128), WINDOW)],
            dst_ref=win.at[s],
            send_sem=xs.at[d - 1],
            recv_sem=xr.at[d - 1],
            device_id=(j, to),
            device_id_type=MESH,
        )
        cp.start()
        sends.append(cp)
    win[s] = rot[:, :, pl.ds(pl.multiple_of(256 * s, 128), WINDOW)]
    for cp in sends:
        cp.wait()
    for other in ring_y:
        pl.semaphore_signal(ysem, inc=1, device_id=other, device_id_type=MESH)
    for c in range(2):
        for t in range(3):
            tile = jnp.concatenate([win[i, c, :, 128 * t : 128 * t + 128] for i in range(4)], axis=0)
            abuf[c, OFF + 128 * t : OFF + 128 * t + 128, :] = tile.T * SCALE

    fine_steps(0, 16, abuf, bbuf, mid, masks)

    pl.semaphore_wait(ysem, 3)
    own = pl.ds(OFF + 64, 256)
    before = pltpu.make_async_remote_copy(
        src_ref=abuf.at[:, own, :], dst_ref=relin, send_sem=rels, recv_sem=relr,
        device_id=(lax.rem(j + 31, 32), s), device_id_type=MESH,
    )
    before.start()

    heun(abuf, mid, cbuf, OFF + 64, 33, 32, masks, COARSE, dst_shift=-(OFF + 64))
    for c in range(2):
        dbuf[c, :, :] = abuf[c, :, :]
    fine_steps(16, 16, dbuf, bbuf, mid, masks)

    for i in range(32):
        for c in range(2):
            rows = pl.ds(8 * i, 8)
            coarse = jnp.where(j > 0, cbuf[c, rows, :], 0.0)
            terms[c, rows, :] = dbuf[c, pl.ds(OFF + 64 + 8 * i, 8), :] - coarse

    def gather(act):
        for part in range(2):
            slot = j - STEPS[0] * part
            for first, end, h in slot_classes(part):

                def pieces(part=part, slot=slot, h=h):
                    for r in range(-2, 10):
                        lo, hi = max(0, B * r - h), min(256, B * r + B + h)
                        if hi <= lo:
                            continue
                        src = terms.at[:, pl.ds(lo, hi - lo), :]
                        dst = got.at[slot, :, pl.ds(lo - (B * r - HALO), hi - lo), :]
                        holder = WORKERS[part][r % 8]
                        to = lax.rem(s + (r // 8) + 4, 4)

                        def remote(src=src, dst=dst, r=r, holder=holder, to=to):
                            act(
                                pltpu.make_async_remote_copy(
                                    src_ref=src, dst_ref=dst, send_sem=gs.at[r + 2], recv_sem=gr.at[slot],
                                    device_id=(holder, to), device_id_type=MESH,
                                ),
                                True,
                            )

                        if 0 <= r < 8:
                            pl.when(j != holder)(remote)

                            @pl.when(j == holder)
                            def _(src=src, dst=dst):
                                act(pltpu.make_async_copy(src, dst, gr.at[slot]), False)
                        else:
                            remote()

                pl.when((slot >= first) & (slot < end))(pieces)

    def start(copy, remote):
        copy.start()

    gather(start)

    before.wait()
    half = sum(jnp.where(j == tm, 1, 0) for tm in WORKERS[1])
    is_worker = sum(jnp.where(j == tm, 1, 0) for tm in WORKERS[0] + WORKERS[1]) > 0
    columns = pl.ds(pl.multiple_of(256 * s, 128), 256)

    def residual():
        for c in range(2):
            for t in range(2):
                rows = pl.ds(OFF + 64 + 128 * t, 128)
                diff = dbuf[c, rows, :] - relin[c, 128 * t : 128 * t + 128, :]
                diff = jnp.where(j < 31, diff, 0.0).T
                for i in range(4):
                    nres[i, c, :, 128 * t : 128 * t + 128] = diff[32 * i : 32 * i + 32, :]
        for i in range(4):
            res_copy(i).start()

    def res_copy(i):
        return pltpu.make_async_remote_copy(
            src_ref=nres.at[i], dst_ref=resid_ref.at[0, :, :, columns], send_sem=ress.at[i], recv_sem=resr,
            device_id=(lax.rem(j + 1, 32), i), device_id_type=MESH,
        )

    def finish(copy, remote):
        if remote:
            copy.wait_send()

    @pl.when(jnp.logical_not(is_worker))
    def _():
        gather(finish)

    @pl.when(jnp.logical_not(is_worker & (half == 0)))
    def _():
        residual()

    r_me = sum(jnp.where(j == tm, r, 0) for table in WORKERS for r, tm in enumerate(table))
    block = 8 * s + r_me
    group = lane // 32

    def pack(n, state, base):
        for c in range(2):
            parts = [state[c, base + 8 * g : base + 8 * g + 8, :] for g in range(4)]
            for i in range(4):
                acc = pltpu.roll(parts[0], (128 - 32 * i) % 128, 1) if i else parts[0]
                for g in range(1, 4):
                    amount = (32 * (g - i)) % 128
                    part = pltpu.roll(parts[g], amount, 1) if amount else parts[g]
                    acc = jnp.where(group == g, part, acc)
                ret[4 * n + i, c, :, :] = acc

    def send_back(part, n):
        row = STEPS[0] * part + n + 1

        def remote(i):
            pltpu.make_async_remote_copy(
                src_ref=ret.at[4 * n + i], dst_ref=back.at[block], send_sem=rets, recv_sem=retr.at[s // 2],
                device_id=(row, i), device_id_type=MESH,
            ).start()

        @pl.when(row != j)
        def _():
            for i in range(4):
                remote(i)

        @pl.when(row == j)
        def _():
            for i in range(4):

                @pl.when(s != i)
                def _(i=i):
                    remote(i)

                @pl.when(s == i)
                def _(i=i):
                    pltpu.make_async_copy(ret.at[4 * n + i], back.at[block], retr.at[s // 2]).start()

    def send_back_from(part, first, end):
        def body(n, _):
            send_back(part, n)
            return 0

        lax.fori_loop(first, end, body, 0)

    def await_terms(part, n):
        h = halo_of(part, n)
        view = got.at[n, :, pl.ds(HALO - h, B + 2 * h), :]
        pltpu.make_async_copy(view, view, gr.at[n]).wait()

    last_state = s1 if STEPS[0] % 2 else s0
    first_h = halo_of(1, 0)

    def hand_over(d):
        lo, hi = max(0, B * d - first_h), min(B, B * d + B + first_h)
        r = r_me + d + 8
        return pltpu.make_async_remote_copy(
            src_ref=last_state.at[:, pl.ds(OFF + HALO + lo, hi - lo), :],
            dst_ref=got.at[0, :, pl.ds(HALO - B * d + lo, hi - lo), :],
            send_sem=hs.at[d + 2], recv_sem=gr.at[0],
            device_id=(pick(WORKERS[1], lax.rem(r, 8)), lax.rem(s + r // 8 + 3, 4)), device_id_type=MESH,
        )

    near = [d for d in (-2, -1, 0, 1, 2) if abs(d) * B < B + first_h]

    def chain(part):
        for n in list(range(1, STEPS[part] + 1)) + [0]:
            await_terms(part, n)
        for c in range(2):
            s0[c, pl.ds(OFF, GW), :] = got[0, c, :GW, :]
        if part == 0:
            pack(0, s0, OFF + HALO)
        for n in range(1, STEPS[part] + 1):
            src, dst = (s0, s1) if n % 2 else (s1, s0)
            left = STEPS[part] - n
            width = B + 4 * left
            heun(
                src, smid, dst, OFF + HALO - 2 * left, (width + 9) // 8, (width + 7) // 8, masks, COARSE,
                extra=lambda c, o, n=n: got[n, c, pl.ds(o - OFF, 8), :],
            )
            if part == 0 and n == STEPS[0]:
                for d in near:
                    hand_over(d).start()
            pack(n, dst, OFF + HALO)
            if part == 1 and n in BATCHES:
                send_back_from(1, max([m for m in BATCHES if m < n], default=0) + 1, n + 1)
        if part == 0:
            send_back_from(0, 0, STEPS[0] + 1)

    for which in range(2):
        pl.when(is_worker & (half == which))(lambda which=which: chain(which))

    @pl.when(is_worker & (half == 0))
    def _():
        residual()

    pltpu.make_async_copy(resid_ref, resid_ref, resr).wait()
    for i in range(4):
        res_copy(i).wait_send()

    @pl.when(is_worker)
    def _():
        gather(finish)

    @pl.when(is_worker & (half == 0))
    def _():
        for d in near:
            hand_over(d).wait_send()

    for which, first, count in ((0, 0, 4 * STEPS[0] + 4), (1, 4, 4 * STEPS[1])):
        inside = (j > 0) & (j < STEPS[0] + 2) if which == 0 else j > STEPS[0] + 1

        @pl.when(is_worker & (half == which) & inside)
        def _(first=first, count=count):
            view = ret.at[pl.ds(first, count - 1)]
            pltpu.make_async_copy(view, view, rets).wait()

        @pl.when(is_worker & (half == which) & jnp.logical_not(inside))
        def _(first=first, count=count):
            view = ret.at[pl.ds(first, count)]
            pltpu.make_async_copy(view, view, rets).wait()

    @pl.when(j == 0)
    def _():
        for c in range(2):
            for t in range(2):
                turned = abuf[c, pl.ds(OFF + 64 + 128 * t, 128), :].T
                for i in range(4):
                    win[i, c, :, 128 * t : 128 * t + 128] = turned[32 * i : 32 * i + 32, :]
        coarse_ref[0, :, :, columns] = win[s, :, :, :256]
        copies = []
        for d in (1, 2, 3):
            to = lax.rem(s + d, 4)
            cp = pltpu.make_async_remote_copy(
                src_ref=win.at[to, :, :, pl.ds(0, 256)], dst_ref=coarse_ref.at[0, :, :, columns],
                send_sem=row0s.at[d - 1], recv_sem=row0r.at[d - 1], device_id=(j, to), device_id_type=MESH,
            )
            cp.start()
            copies.append(cp)
        for cp in copies:
            cp.wait()

    @pl.when(j > 0)
    def _():
        for turn in range(2):
            half_at = lax.rem(s // 2 + turn, 2)
            view = back.at[pl.ds(16 * half_at, 16)]
            pltpu.make_async_copy(view, view, retr.at[half_at]).wait()
            for c in range(2):
                strips = []
                for e in range(4):
                    packed = [back[16 * half_at + 4 * k + e, c, :, :] for k in range(4)]
                    for g in range(4):
                        acc = None
                        for k in range(4):
                            amount = (32 * (k - g)) % 128
                            part = pltpu.roll(packed[k], amount, 1) if amount else packed[k]
                            acc = part if acc is None else jnp.where(group == k, part, acc)
                        strips.append(acc)
                square = jnp.concatenate(strips, axis=0).T
                for k in range(4):
                    tile = pl.ds(pl.multiple_of(512 * half_at + 128 * k, 128), 128)
                    coarse_ref[0, c, :, tile] = square[32 * k : 32 * k + 32, :]


def on_device(iterate):
    vmem = pl.BlockSpec(memory_space=pltpu.VMEM)
    dma = pltpu.SemaphoreType.DMA
    shape = jax.ShapeDtypeStruct((1, 2, 32, 1024), F32)
    coarse, resid = pl.pallas_call(
        kernel,
        out_shape=(shape, shape),
        in_specs=[pl.BlockSpec(memory_space=pl.ANY)],
        out_specs=(vmem, vmem),
        scratch_shapes=[
            pltpu.VMEM((2, 32, 1024), F32),
            pltpu.VMEM((2, 32, 1152), F32),
            pltpu.VMEM((4, 2, 32, WINDOW), F32),
            pltpu.VMEM((2, ROWS, 128), F32),
            pltpu.VMEM((2, ROWS, 128), F32),
            pltpu.VMEM((2, ROWS, 128), F32),
            pltpu.VMEM((2, ROWS, 128), F32),
            pltpu.VMEM((2, 256, 128), F32),
            pltpu.VMEM((2, 256, 128), F32),
            pltpu.VMEM((2, 256, 128), F32),
            pltpu.VMEM((max(STEPS) + 1, 2, GW + 16, 128), F32),
            pltpu.VMEM((2, GW + 32, 128), F32),
            pltpu.VMEM((2, GW + 32, 128), F32),
            pltpu.VMEM((2, GW + 32, 128), F32),
            pltpu.VMEM((4 * max(STEPS) + 4, 2, 8, 128), F32),
            pltpu.VMEM((32, 2, 8, 128), F32),
            pltpu.VMEM((4, 2, 32, 256), F32),
            dma, dma((3,)), dma((3,)),
            pltpu.SemaphoreType.REGULAR,
            dma, dma,
            dma((12,)), dma((max(STEPS) + 1,)), dma((5,)),
            dma, dma((2,)),
            dma((4,)), dma,
            dma((3,)), dma((3,)),
        ],
        compiler_params=pltpu.CompilerParams(
            collective_id=0, has_side_effects=True, vmem_limit_bytes=48 * 2**20
        ),
    )(iterate)
    return coarse * (1.0 / SCALE), resid * (1.0 / SCALE)


def solution(mesh):
    spec = P("tm", None, "space", None)
    return jax.shard_map(on_device, mesh=mesh, in_specs=(spec,), out_specs=(spec, spec), check_vma=False)
```
